32 devices in a mesh: blk: 8 (over z, x), wn: 4 (over y, core).
Axes of the slice: x: 2, y: 2, z: 4, core: 2. Of those that a mesh axis runs over, the one named last changes fastest.
Arguments:
- species_molar_share: float32 [11, 64, 2, 1024], P(None, 'wn', None, 'blk'), may hold values from 0.01 to 1
- flow_speed_vector: float32 [2, 64, 2, 1024], P(None, 'wn', None, 'blk'), may hold values from -6 to 6
- thermal_level: float32 [64, 2, 1024], P('wn', None, 'blk'), may hold values from 0.5 to 2
- shear_collision_terms: float32 [11, 11], replicated, may hold values from 1 to 2
- thermal_collision_terms: float32 [11, 11], replicated, may hold values from 1 to 2
Outputs:
- final_state: float32 [14, 64, 2, 1024], P(None, 'wn', None, 'blk')
- last_residual: float32 [14, 64, 2, 1024], P(None, 'wn', None, 'blk')
The draws below stay inside these ranges and needn't reach their ends.
All inputs are finite; a program needn't handle non-finite values.
Results may differ from the reference program's by a relative error of at most 0.00005.
Values sent between devices are 32-bit elements; how exact they have to be, the bound alone decides.
A program may use at most 64 MiB of HBM per device.

```python
import math
import jax
import jax.numpy as jnp
import numpy as np
from jax import lax

NSPEC = 11
DOWNWIND_SPAN = 1024
WALLWARD_SPAN = 64


def log_spread(key, extent, lower_end, upper_end):
    values = jnp.exp(jax.random.uniform(key, extent, jnp.float32, math.log(lower_end), math.log(upper_end)))
    return jnp.minimum(jnp.maximum(values, lower_end), upper_end)


def draw_thermal_level(key, part):
    key = jax.random.fold_in(key, 11)
    extent = (WALLWARD_SPAN, 2, DOWNWIND_SPAN)
    return log_spread(key, extent, 0.5, 2.0)


def draw_shear_collision_terms(key, part):
    key = jax.random.fold_in(key, 23)
    return log_spread(key, (NSPEC, NSPEC), 1.0, 2.0)


def draw_thermal_collision_terms(key, part):
    key = jax.random.fold_in(key, 37)
    return log_spread(key, (NSPEC, NSPEC), 1.0, 2.0)


def block_levels(own_key, shape, shards, smallest, largest):
    loudness = 1.0
    for axis_at, blocks in shards:
        draws = jax.random.uniform(jax.random.fold_in(jax.random.fold_in(own_key, 6), axis_at), (blocks,), jnp.float32, smallest / len(shards), largest / len(shards))
        loudness = loudness * jnp.repeat(jnp.exp(draws), shape[axis_at] // blocks).reshape((-1,) + (1,) * (len(shape) - 1 - axis_at))
    return loudness


def scatter_about(key, shape, deviation, limit, cuts=(), kind=jnp.bfloat16):
    entries = deviation * jax.random.normal(key, shape, jnp.float32)
    if cuts:
        entries = entries * block_levels(key, shape, cuts, -0.22, 0.18)
    return jnp.clip(entries, -limit, limit).astype(kind)


def setup_inputs(seed: int = 0) -> dict:
    key_of = jax.random.split(jax.random.key(seed), 6)
    return {
        "species_molar_share": jnp.clip(jnp.exp(math.log(1.0) - 4.6051702 * jax.random.uniform(key_of[0], (NSPEC, WALLWARD_SPAN, 2, DOWNWIND_SPAN), jnp.float32) ** block_levels(key_of[0], (NSPEC, WALLWARD_SPAN, 2, DOWNWIND_SPAN), ((1, 4), (3, 8)), -0.2, 0.2)), 0.01, 1.0),
        "flow_speed_vector": scatter_about(key_of[1], (2, WALLWARD_SPAN, 2, DOWNWIND_SPAN), 1.0, 6.0, ((1, 4), (3, 8)), jnp.float32),
        "thermal_level": draw_thermal_level(jax.random.fold_in(key_of[5], 71), 0),
        "shear_collision_terms": draw_shear_collision_terms(jax.random.fold_in(key_of[5], 71), 0),
        "thermal_collision_terms": draw_thermal_collision_terms(jax.random.fold_in(key_of[5], 71), 0),
    }


MASSES = np.array([28.0, 32.0, 30.0, 14.0, 16.0, 28.0, 32.0, 30.0, 14.0, 16.0, 0.00055]) / 28.0


def properties(padded, shear_collision_terms, thermal_collision_terms):
    fractions = padded[:11]
    heat = padded[13]
    denom_visc = jnp.einsum("sr,rjki->sjki", shear_collision_terms, fractions, precision=lax.Precision.HIGHEST)
    denom_cond = jnp.einsum("sr,rjki->sjki", thermal_collision_terms, fractions, precision=lax.Precision.HIGHEST)
    mixture_viscosity = heat ** 0.7 * jnp.sum(fractions * MASSES[:, None, None, None] / denom_visc, axis=0)
    conduct = heat ** 0.5 * jnp.sum(fractions / denom_cond, axis=0)
    return mixture_viscosity, conduct


def shifted(field, down, across):
    rows = field.shape[-3]
    cols = field.shape[-1]
    return field[..., 1 + down:rows - 1 + down, :, 1 + across:cols - 1 + across]


def diffuse(padded, coeff):
    center_c = shifted(coeff, 0, 0)
    center_face = shifted(padded, 0, 0)
    total = jnp.zeros_like(center_face)
    for down, across in ((1, 0), (-1, 0), (0, 1), (0, -1)):
        total = total + 0.5 * (center_c + shifted(coeff, down, across)) * (shifted(padded, down, across) - center_face)
    return total


def residual_of(padded, mixture_viscosity, conduct):
    return jnp.concatenate([diffuse(padded[:11], conduct), diffuse(padded[11:13], mixture_viscosity), diffuse(padded[13:], conduct)], axis=0)


def pad_state(state):
    rows_done = jnp.concatenate([state[:, 1:2, ::-1, :], state, state[:, -1:, :, :]], axis=1)
    return jnp.concatenate([rows_done[..., :1], rows_done, rows_done[:, :, ::-1, -1:]], axis=3)


def evaluate(state, shear_collision_terms, thermal_collision_terms):
    padded = pad_state(state)
    mixture_viscosity, conduct = properties(padded, shear_collision_terms, thermal_collision_terms)
    return residual_of(padded, mixture_viscosity, conduct)


def reference(species_molar_share, flow_speed_vector, thermal_level, shear_collision_terms, thermal_collision_terms):
    step = 0.16
    first_position = jnp.concatenate([species_molar_share, flow_speed_vector, thermal_level[None]], axis=0)
    first = first_position + step * evaluate(first_position, shear_collision_terms, thermal_collision_terms)
    second = 0.75 * first_position + 0.25 * (first + step * evaluate(first, shear_collision_terms, thermal_collision_terms))
    last_residual = evaluate(second, shear_collision_terms, thermal_collision_terms)
    final_state = first_position / 3.0 + 2.0 / 3.0 * (second + step * last_residual)
    return final_state, last_residual
```

```python
import jax
import jax.numpy as jnp
import numpy as np
from jax import lax
from jax.experimental import pallas as pl
from jax.experimental.pallas import tpu as pltpu
from jax.sharding import PartitionSpec as P

MASSES = np.array([28.0, 32.0, 30.0, 14.0, 16.0, 28.0, 32.0, 30.0, 14.0, 16.0, 0.00055]) / 28.0
NS = 11
NV = 14
STEP = 0.16
VERTICAL = ((1, 0), (-1, 0))
SIDEWAYS = ((0, 1), (0, -1), (1, 1), (1, -1), (-1, 1), (-1, -1))
EDGE_TILES = 4


def roll(x, shift, axis):
    size = x.shape[axis]
    shift = shift % size
    return x if shift == 0 else pltpu.roll(x, shift, axis)


def lanes_of(shape):
    return lax.broadcasted_iota(jnp.int32, shape, len(shape) - 1)


def rows_of(shape):
    return lax.broadcasted_iota(jnp.int32, shape, len(shape) - 2)


def exchange_kernel(
    species, velocity, heat, vert, side, own, out_v, send_v, recv_v, send_s, recv_s
):
    wn = lax.axis_index("wn")
    blk = lax.axis_index("blk")
    wn_count = lax.axis_size("wn")
    blk_count = lax.axis_size("blk")

    def exists(dw, db):
        checks = []
        if dw:
            checks.append(wn < wn_count - 1 if dw > 0 else wn > 0)
        if db:
            checks.append(blk < blk_count - 1 if db > 0 else blk > 0)
        return checks[0] if len(checks) == 1 else jnp.logical_and(*checks)

    def device(dw, db):
        return {"wn": wn + dw, "blk": blk + db}

    barrier = pltpu.get_barrier_semaphore()
    for dw, db in VERTICAL + SIDEWAYS:

        @pl.when(exists(dw, db))
        def _(dw=dw, db=db):
            pl.semaphore_signal(
                barrier, inc=1, device_id=device(dw, db), device_id_type=pl.DeviceIdType.MESH
            )

    def tile(v, g):
        rows = pl.ds(8 * g, 8)
        if v < NS:
            return species[v, rows]
        if v < NS + 2:
            return velocity[v - NS, rows]
        return heat[rows]

    slot = lanes_of((8, 128)) // 8
    for t in range(EDGE_TILES):
        packed = jnp.zeros((8, 128), jnp.float32)
        for v in range(4 * t, min(4 * t + 4, NV)):
            for g in range(4):
                at = 4 * (v % 4) + g
                packed = jnp.where(slot == at, roll(tile(v, g), 8 * at + 3, 1), packed)
        own[t] = packed
        out_v[0, NV + t] = packed
        out_v[1, NV + t] = packed
    for v in range(NV):
        out_v[0, v] = tile(v, 3)
        out_v[1, v] = tile(v, 0)

    along_wn = 1 + (wn > 0).astype(jnp.int32) + (wn < wn_count - 1).astype(jnp.int32)
    along_blk = 1 + (blk > 0).astype(jnp.int32) + (blk < blk_count - 1).astype(jnp.int32)
    pl.semaphore_wait(barrier, along_wn * along_blk - 1)

    copies = []
    for n, (dw, db) in enumerate(VERTICAL):
        copies.append((dw, db, pltpu.make_async_remote_copy(
            src_ref=out_v.at[n], dst_ref=vert.at[n], send_sem=send_v.at[n], recv_sem=recv_v.at[n],
            device_id=device(dw, db), device_id_type=pl.DeviceIdType.MESH)))
    for n, (dw, db) in enumerate(SIDEWAYS):
        copies.append((dw, db, pltpu.make_async_remote_copy(
            src_ref=own, dst_ref=side.at[n], send_sem=send_s.at[n], recv_sem=recv_s.at[n],
            device_id=device(dw, db), device_id_type=pl.DeviceIdType.MESH)))
    for dw, db, copy in copies:
        pl.when(exists(dw, db))(copy.start)
    for dw, db, copy in copies:
        pl.when(exists(-dw, -db))(copy.wait_recv)
    for dw, db, copy in copies:
        pl.when(exists(dw, db))(copy.wait_send)


def sections_kernel(
    shear, thermal, species, velocity, heat, vert, side, own, final, residual, now, first, kept
):
    wn = lax.axis_index("wn")
    blk = lax.axis_index("blk")
    at_bottom = wn == 0
    at_top = wn == lax.axis_size("wn") - 1
    at_wake = blk == 0
    at_nose = blk == lax.axis_size("blk") - 1
    lane = lanes_of((8, 128))
    sub = rows_of((8, 128))
    c = lane % 8
    is_left = lane < 64
    group = (lane % 64) // 8

    for v in range(NV):
        now[v, 0:8] = vert[0, v]
        now[v, 40:48] = vert[1, v]
    now[0:NS, 8:40] = species[...]
    now[NS:NS + 2, 8:40] = velocity[...]
    now[NV - 1, 8:40] = heat[...]
    for t in range(EDGE_TILES):
        from_left, from_right = c < 3, c >= 3
        mid, low, high = own[t], vert[0, NV + t], vert[1, NV + t]
        left_mid = jnp.where(from_left, side[0, t], mid)
        left_low = jnp.where(from_left, side[2, t], low)
        left_high = jnp.where(from_left, side[4, t], high)
        right_mid = jnp.where(from_right, side[1, t], mid)
        right_low = jnp.where(from_right, side[3, t], low)
        right_high = jnp.where(from_right, side[5, t], high)
        for v in range(4 * t, min(4 * t + 4, NV)):
            base = 32 * (v % 4)
            left = roll(left_mid, 8 - base, 1)
            left = jnp.where(group == 0, roll(left_low, -24 - base, 1), left)
            left = jnp.where(group == 5, roll(left_high, 40 - base, 1), left)
            right = roll(right_mid, 72 - base, 1)
            right = jnp.where(group == 0, roll(right_low, 40 - base, 1), right)
            right = jnp.where(group == 5, roll(right_high, 104 - base, 1), right)
            now[v, 48:56] = jnp.where(is_left, left, right)
    first[...] = now[...]

    bottom_6 = (sub == 6) & at_bottom
    bottom_7 = (sub == 7) & at_bottom
    top_01 = (sub < 2) & at_top
    patch_bottom_6 = bottom_6 & (group == 0)
    patch_bottom_7 = bottom_7 & (group == 0)
    patch_top = top_01 & (group == 5)
    patch_wake = is_left & (c == 2) & at_wake
    patch_nose = (~is_left) & (c == 3) & at_nose
    even = sub % 2 == 0

    def ghost(v):
        inner = now[v, 8:16]
        below = now[v, 0:8]
        below = jnp.where(bottom_6, roll(inner, 3, 0), below)
        now[v, 0:8] = jnp.where(bottom_7, roll(inner, 5, 0), below)
        now[v, 40:48] = jnp.where(top_01, roll(now[v, 32:40], 2, 0), now[v, 40:48])
        patch = now[v, 48:56]
        inner = roll(patch, -8, 1)
        patch = jnp.where(patch_bottom_6, roll(inner, 3, 0), patch)
        patch = jnp.where(patch_bottom_7, roll(inner, 5, 0), patch)
        patch = jnp.where(patch_top, roll(roll(patch, 8, 1), 2, 0), patch)
        patch = jnp.where(patch_wake, roll(patch, -1, 1), patch)
        inner = roll(patch, 1, 1)
        patch = jnp.where(
            patch_nose, jnp.where(even, roll(inner, -1, 0), roll(inner, 1, 0)), patch
        )
        now[v, 48:56] = patch

    def patch_up(x):
        y = roll(x, -2, 0)
        return jnp.where(sub < 6, y, roll(y, -8, 1))

    def patch_down(x):
        y = roll(x, 2, 0)
        return jnp.where(sub >= 2, y, roll(y, 8, 1))

    main_lane = lanes_of((48, 128))
    last_lane = main_lane == 127
    zero_lane = main_lane == 0

    def section(number, old_share, new_share):
        for v in range(NV):
            ghost(v)
        visc = jnp.zeros((56, 128), jnp.float32)
        cond = jnp.zeros((56, 128), jnp.float32)
        for s in range(NS):
            den_visc = shear[s, 0] * now[0]
            den_cond = thermal[s, 0] * now[0]
            for r in range(1, NS):
                den_visc = den_visc + shear[s, r] * now[r]
                den_cond = den_cond + thermal[s, r] * now[r]
            visc = visc + (float(MASSES[s]) * now[s]) / den_visc
            cond = cond + now[s] / den_cond
        temperature = now[NV - 1]
        kept[0] = jnp.exp(0.7 * jnp.log(temperature)) * visc
        kept[1] = jnp.sqrt(temperature) * cond
        for n in range(2):
            main, patch = kept[n, 0:48], kept[n, 48:56]
            kept[2 + n, 0:48] = 0.5 * (main + roll(main, -2, 0))
            kept[2 + n, 48:56] = 0.5 * (patch + patch_up(patch))
            kept[4 + n, 0:48] = 0.5 * (main + roll(main, -1, 1))
            kept[4 + n, 48:56] = 0.5 * (patch + roll(patch, -1, 1))
        for v in range(NV):
            n = 0 if NS <= v < NS + 2 else 1
            main, patch = now[v, 0:48], now[v, 48:56]
            across_patch = kept[4 + n, 48:56] * (roll(patch, -1, 1) - patch)
            seam = jnp.where(c == 1, roll(across_patch, 63, 1), across_patch)
            closing = jnp.concatenate([roll(seam, -8 * g - 2, 1) for g in range(6)], axis=0)
            across = kept[4 + n, 0:48] * (roll(main, -1, 1) - main)
            before = jnp.where(zero_lane, closing, roll(across, 1, 1))
            across = jnp.where(last_lane, closing, across)
            down = kept[2 + n, 0:48] * (roll(main, -2, 0) - main)
            change = (across - before) + (down - roll(down, 2, 0))
            if number < 2:
                down_patch = kept[2 + n, 48:56] * (patch_up(patch) - patch)
                change_patch = (across_patch - roll(across_patch, 1, 1)) + (
                    down_patch - patch_down(down_patch)
                )
                new_main = main + STEP * change
                new_patch = patch + STEP * change_patch
                if old_share:
                    new_main = old_share * first[v, 0:48] + new_share * new_main
                    new_patch = old_share * first[v, 48:56] + new_share * new_patch
                now[v, 0:48] = new_main
                now[v, 48:56] = new_patch
            else:
                inner = change[8:40]
                residual[v] = inner
                final[v] = old_share * first[v, 8:40] + new_share * (main[8:40] + STEP * inner)

    section(0, 0.0, 1.0)
    section(1, 0.75, 0.25)
    section(2, 1.0 / 3.0, 2.0 / 3.0)


def local(species, velocity, heat, shear, thermal):
    layers = species.shape[1]
    columns = species.shape[3]
    assert (layers, columns) == (16, 128)
    rows = 2 * layers
    species = species.reshape(NS, rows, columns)
    velocity = velocity.reshape(2, rows, columns)
    heat = heat.reshape(rows, columns)
    f32 = jnp.float32
    vmem = pl.BlockSpec(memory_space=pltpu.VMEM)
    smem = pl.BlockSpec(memory_space=pltpu.SMEM)
    tiles = NV + EDGE_TILES
    vert, side, own = pl.pallas_call(
        exchange_kernel,
        out_shape=(
            jax.ShapeDtypeStruct((2, tiles, 8, columns), f32),
            jax.ShapeDtypeStruct((6, EDGE_TILES, 8, columns), f32),
            jax.ShapeDtypeStruct((EDGE_TILES, 8, columns), f32),
        ),
        in_specs=[vmem] * 3,
        out_specs=(vmem,) * 3,
        scratch_shapes=[
            pltpu.VMEM((2, tiles, 8, columns), f32),
            pltpu.SemaphoreType.DMA((2,)),
            pltpu.SemaphoreType.DMA((2,)),
            pltpu.SemaphoreType.DMA((6,)),
            pltpu.SemaphoreType.DMA((6,)),
        ],
        compiler_params=pltpu.CompilerParams(collective_id=0, has_side_effects=True),
        name="exchange",
    )(species, velocity, heat)
    shape = jax.ShapeDtypeStruct((NV, rows, columns), f32)
    final, residual = pl.pallas_call(
        sections_kernel,
        out_shape=(shape, shape),
        in_specs=[smem] * 2 + [vmem] * 6,
        out_specs=(vmem,) * 2,
        scratch_shapes=[
            pltpu.VMEM((NV, rows + 24, columns), f32),
            pltpu.VMEM((NV, rows + 24, columns), f32),
            pltpu.VMEM((6, rows + 24, columns), f32),
        ],
        name="sections",
    )(shear, thermal, species, velocity, heat, vert, side, own)
    whole = (NV, layers, 2, columns)
    return final.reshape(whole), residual.reshape(whole)


def solution(mesh):
    return jax.shard_map(
        local,
        mesh=mesh,
        in_specs=(
            P(None, "wn", None, "blk"),
            P(None, "wn", None, "blk"),
            P("wn", None, "blk"),
            P(),
            P(),
        ),
        out_specs=(P(None, "wn", None, "blk"), P(None, "wn", None, "blk")),
        check_vma=False,
    )
```

```python
import jax
import jax.numpy as jnp
import numpy as np
from jax import lax
from jax.experimental import pallas as pl
from jax.experimental.pallas import tpu as pltpu
from jax.sharding import PartitionSpec as P

MASSES = np.array([28.0, 32.0, 30.0, 14.0, 16.0, 28.0, 32.0, 30.0, 14.0, 16.0, 0.00055]) / 28.0
NS = 11
NV = 14
STEP = 0.16
VERTICAL = ((1, 0), (-1, 0))
SIDEWAYS = ((0, 1), (0, -1), (1, 1), (1, -1), (-1, 1), (-1, -1))
EDGE_TILES = 4


def roll(x, shift, axis):
    size = x.shape[axis]
    shift = shift % size
    return x if shift == 0 else pltpu.roll(x, shift, axis)


def inverse(x):
    guess = pl.reciprocal(x, approx=True)
    return guess * (2.0 - x * guess)


def lanes_of(shape):
    return lax.broadcasted_iota(jnp.int32, shape, len(shape) - 1)


def rows_of(shape):
    return lax.broadcasted_iota(jnp.int32, shape, len(shape) - 2)


def exchange_kernel(
    species, velocity, heat, vert, side, own, out_v, send_v, recv_v, send_s, recv_s
):
    wn = lax.axis_index("wn")
    blk = lax.axis_index("blk")
    wn_count = lax.axis_size("wn")
    blk_count = lax.axis_size("blk")

    def exists(dw, db):
        checks = []
        if dw:
            checks.append(wn < wn_count - 1 if dw > 0 else wn > 0)
        if db:
            checks.append(blk < blk_count - 1 if db > 0 else blk > 0)
        return checks[0] if len(checks) == 1 else jnp.logical_and(*checks)

    def device(dw, db):
        return {"wn": wn + dw, "blk": blk + db}

    barrier = pltpu.get_barrier_semaphore()
    for dw, db in VERTICAL + SIDEWAYS:

        @pl.when(exists(dw, db))
        def _(dw=dw, db=db):
            pl.semaphore_signal(
                barrier, inc=1, device_id=device(dw, db), device_id_type=pl.DeviceIdType.MESH
            )

    def tile(v, g):
        rows = pl.ds(8 * g, 8)
        if v < NS:
            return species[v, rows]
        if v < NS + 2:
            return velocity[v - NS, rows]
        return heat[rows]

    slot = lanes_of((8, 128)) // 8
    for t in range(EDGE_TILES):
        packed = jnp.zeros((8, 128), jnp.float32)
        for v in range(4 * t, min(4 * t + 4, NV)):
            for g in range(4):
                at = 4 * (v % 4) + g
                packed = jnp.where(slot == at, roll(tile(v, g), 8 * at + 3, 1), packed)
        own[t] = packed
        out_v[0, NV + t] = packed
        out_v[1, NV + t] = packed
    for v in range(NV):
        out_v[0, v] = tile(v, 3)
        out_v[1, v] = tile(v, 0)

    along_wn = 1 + (wn > 0).astype(jnp.int32) + (wn < wn_count - 1).astype(jnp.int32)
    along_blk = 1 + (blk > 0).astype(jnp.int32) + (blk < blk_count - 1).astype(jnp.int32)
    pl.semaphore_wait(barrier, along_wn * along_blk - 1)

    copies = []
    for n, (dw, db) in enumerate(VERTICAL):
        copies.append((dw, db, pltpu.make_async_remote_copy(
            src_ref=out_v.at[n], dst_ref=vert.at[n], send_sem=send_v.at[n], recv_sem=recv_v.at[n],
            device_id=device(dw, db), device_id_type=pl.DeviceIdType.MESH)))
    for n, (dw, db) in enumerate(SIDEWAYS):
        copies.append((dw, db, pltpu.make_async_remote_copy(
            src_ref=own, dst_ref=side.at[n], send_sem=send_s.at[n], recv_sem=recv_s.at[n],
            device_id=device(dw, db), device_id_type=pl.DeviceIdType.MESH)))
    for dw, db, copy in copies:
        pl.when(exists(dw, db))(copy.start)
    for dw, db, copy in copies:
        pl.when(exists(-dw, -db))(copy.wait_recv)
    for dw, db, copy in copies:
        pl.when(exists(dw, db))(copy.wait_send)


def sections_kernel(
    shear, thermal, species, velocity, heat, vert, side, own, final, residual, now, first, kept
):
    wn = lax.axis_index("wn")
    blk = lax.axis_index("blk")
    at_bottom = wn == 0
    at_top = wn == lax.axis_size("wn") - 1
    at_wake = blk == 0
    at_nose = blk == lax.axis_size("blk") - 1
    lane = lanes_of((8, 128))
    sub = rows_of((8, 128))
    c = lane % 8
    is_left = lane < 64
    group = (lane % 64) // 8

    for v in range(NV):
        now[v, 0:8] = vert[0, v]
        now[v, 40:48] = vert[1, v]
    now[0:NS, 8:40] = species[...]
    now[NS:NS + 2, 8:40] = velocity[...]
    now[NV - 1, 8:40] = heat[...]
    for t in range(EDGE_TILES):
        from_left, from_right = c < 3, c >= 3
        mid, low, high = own[t], vert[0, NV + t], vert[1, NV + t]
        left_mid = jnp.where(from_left, side[0, t], mid)
        left_low = jnp.where(from_left, side[2, t], low)
        left_high = jnp.where(from_left, side[4, t], high)
        right_mid = jnp.where(from_right, side[1, t], mid)
        right_low = jnp.where(from_right, side[3, t], low)
        right_high = jnp.where(from_right, side[5, t], high)
        for v in range(4 * t, min(4 * t + 4, NV)):
            base = 32 * (v % 4)
            left = roll(left_mid, 8 - base, 1)
            left = jnp.where(group == 0, roll(left_low, -24 - base, 1), left)
            left = jnp.where(group == 5, roll(left_high, 40 - base, 1), left)
            right = roll(right_mid, 72 - base, 1)
            right = jnp.where(group == 0, roll(right_low, 40 - base, 1), right)
            right = jnp.where(group == 5, roll(right_high, 104 - base, 1), right)
            now[v, 48:56] = jnp.where(is_left, left, right)
    first[...] = now[...]

    bottom_6 = (sub == 6) & at_bottom
    bottom_7 = (sub == 7) & at_bottom
    top_01 = (sub < 2) & at_top
    patch_bottom_6 = bottom_6 & (group == 0)
    patch_bottom_7 = bottom_7 & (group == 0)
    patch_top = top_01 & (group == 5)
    patch_wake = is_left & (c == 2) & at_wake
    patch_nose = (~is_left) & (c == 3) & at_nose
    even = sub % 2 == 0

    def ghost(v):
        inner = now[v, 8:16]
        below = now[v, 0:8]
        below = jnp.where(bottom_6, roll(inner, 3, 0), below)
        now[v, 0:8] = jnp.where(bottom_7, roll(inner, 5, 0), below)
        now[v, 40:48] = jnp.where(top_01, roll(now[v, 32:40], 2, 0), now[v, 40:48])
        patch = now[v, 48:56]
        inner = roll(patch, -8, 1)
        patch = jnp.where(patch_bottom_6, roll(inner, 3, 0), patch)
        patch = jnp.where(patch_bottom_7, roll(inner, 5, 0), patch)
        patch = jnp.where(patch_top, roll(roll(patch, 8, 1), 2, 0), patch)
        patch = jnp.where(patch_wake, roll(patch, -1, 1), patch)
        inner = roll(patch, 1, 1)
        patch = jnp.where(
            patch_nose, jnp.where(even, roll(inner, -1, 0), roll(inner, 1, 0)), patch
        )
        now[v, 48:56] = patch

    def patch_up(x):
        y = roll(x, -2, 0)
        return jnp.where(sub < 6, y, roll(y, -8, 1))

    def patch_down(x):
        y = roll(x, 2, 0)
        return jnp.where(sub >= 2, y, roll(y, 8, 1))

    main_lane = lanes_of((48, 128))
    last_lane = main_lane == 127
    zero_lane = main_lane == 0

    def section(number, old_share, new_share):
        for v in range(NV):
            ghost(v)
        if number == 0:
            cells = [now[r] for r in range(NV)]
        else:
            cells = [
                jnp.concatenate(
                    [now[r, 8:40], now[r, 48:56], jnp.where(sub >= 4, now[r, 0:8], now[r, 40:48])],
                    axis=0,
                )
                for r in range(NV)
            ]
        visc = cond = None
        for s in range(NS):
            den_visc = shear[s, 0] * cells[0]
            den_cond = thermal[s, 0] * cells[0]
            for r in range(1, NS):
                den_visc = den_visc + shear[s, r] * cells[r]
                den_cond = den_cond + thermal[s, r] * cells[r]
            visc_s = (float(MASSES[s]) * cells[s]) * inverse(den_visc)
            cond_s = cells[s] * inverse(den_cond)
            visc = visc_s if s == 0 else visc + visc_s
            cond = cond_s if s == 0 else cond + cond_s
        temperature = cells[NV - 1]
        visc = jnp.exp(0.7 * jnp.log(temperature)) * visc
        cond = jnp.sqrt(temperature) * cond
        for n, k in enumerate((visc, cond)):
            if number == 0:
                kept[n] = k
            else:
                kept[n, 8:40] = k[0:32]
                kept[n, 48:56] = k[32:40]
                kept[n, 0:8] = k[40:48]
                kept[n, 40:48] = k[40:48]
        for n in range(2):
            main, patch = kept[n, 0:48], kept[n, 48:56]
            kept[2 + n, 0:48] = 0.5 * (main + roll(main, -2, 0))
            kept[2 + n, 48:56] = 0.5 * (patch + patch_up(patch))
            kept[4 + n, 0:48] = 0.5 * (main + roll(main, -1, 1))
            kept[4 + n, 48:56] = 0.5 * (patch + roll(patch, -1, 1))
        for v in range(NV):
            n = 0 if NS <= v < NS + 2 else 1
            main, patch = now[v, 0:48], now[v, 48:56]
            across_patch = kept[4 + n, 48:56] * (roll(patch, -1, 1) - patch)
            seam = jnp.where(c == 1, roll(across_patch, 63, 1), across_patch)
            closing = jnp.concatenate([roll(seam, -8 * g - 2, 1) for g in range(6)], axis=0)
            across = kept[4 + n, 0:48] * (roll(main, -1, 1) - main)
            before = jnp.where(zero_lane, closing, roll(across, 1, 1))
            across = jnp.where(last_lane, closing, across)
            down = kept[2 + n, 0:48] * (roll(main, -2, 0) - main)
            change = (across - before) + (down - roll(down, 2, 0))
            if number < 2:
                down_patch = kept[2 + n, 48:56] * (patch_up(patch) - patch)
                change_patch = (across_patch - roll(across_patch, 1, 1)) + (
                    down_patch - patch_down(down_patch)
                )
                new_main = main + STEP * change
                new_patch = patch + STEP * change_patch
                if old_share:
                    new_main = old_share * first[v, 0:48] + new_share * new_main
                    new_patch = old_share * first[v, 48:56] + new_share * new_patch
                now[v, 0:48] = new_main
                now[v, 48:56] = new_patch
            else:
                inner = change[8:40]
                residual[v] = inner
                final[v] = old_share * first[v, 8:40] + new_share * (main[8:40] + STEP * inner)

    section(0, 0.0, 1.0)
    section(1, 0.75, 0.25)
    section(2, 1.0 / 3.0, 2.0 / 3.0)


def local(species, velocity, heat, shear, thermal):
    layers = species.shape[1]
    columns = species.shape[3]
    assert (layers, columns) == (16, 128)
    rows = 2 * layers
    species = species.reshape(NS, rows, columns)
    velocity = velocity.reshape(2, rows, columns)
    heat = heat.reshape(rows, columns)
    f32 = jnp.float32
    vmem = pl.BlockSpec(memory_space=pltpu.VMEM)
    smem = pl.BlockSpec(memory_space=pltpu.SMEM)
    tiles = NV + EDGE_TILES
    vert, side, own = pl.pallas_call(
        exchange_kernel,
        out_shape=(
            jax.ShapeDtypeStruct((2, tiles, 8, columns), f32),
            jax.ShapeDtypeStruct((6, EDGE_TILES, 8, columns), f32),
            jax.ShapeDtypeStruct((EDGE_TILES, 8, columns), f32),
        ),
        in_specs=[vmem] * 3,
        out_specs=(vmem,) * 3,
        scratch_shapes=[
            pltpu.VMEM((2, tiles, 8, columns), f32),
            pltpu.SemaphoreType.DMA((2,)),
            pltpu.SemaphoreType.DMA((2,)),
            pltpu.SemaphoreType.DMA((6,)),
            pltpu.SemaphoreType.DMA((6,)),
        ],
        compiler_params=pltpu.CompilerParams(collective_id=0, has_side_effects=True),
        name="exchange",
    )(species, velocity, heat)
    shape = jax.ShapeDtypeStruct((NV, rows, columns), f32)
    final, residual = pl.pallas_call(
        sections_kernel,
        out_shape=(shape, shape),
        in_specs=[smem] * 2 + [vmem] * 6,
        out_specs=(vmem,) * 2,
        scratch_shapes=[
            pltpu.VMEM((NV, rows + 24, columns), f32),
            pltpu.VMEM((NV, rows + 24, columns), f32),
            pltpu.VMEM((6, rows + 24, columns), f32),
        ],
        name="sections",
    )(shear, thermal, species, velocity, heat, vert, side, own)
    whole = (NV, layers, 2, columns)
    return final.reshape(whole), residual.reshape(whole)


def solution(mesh):
    return jax.shard_map(
        local,
        mesh=mesh,
        in_specs=(
            P(None, "wn", None, "blk"),
            P(None, "wn", None, "blk"),
            P("wn", None, "blk"),
            P(),
            P(),
        ),
        out_specs=(P(None, "wn", None, "blk"), P(None, "wn", None, "blk")),
        check_vma=False,
    )
```

```python
import jax
import jax.numpy as jnp
import numpy as np
from jax import lax
from jax.experimental import pallas as pl
from jax.experimental.pallas import tpu as pltpu
from jax.sharding import PartitionSpec as P

MASSES = np.array([28.0, 32.0, 30.0, 14.0, 16.0, 28.0, 32.0, 30.0, 14.0, 16.0, 0.00055]) / 28.0
NS = 11
NV = 14
STEP = 0.16
VERTICAL = ((1, 0), (-1, 0))
SIDEWAYS = ((0, 1), (0, -1), (1, 1), (1, -1), (-1, 1), (-1, -1))
EDGE_TILES = 4


def roll(x, shift, axis):
    size = x.shape[axis]
    shift = shift % size
    return x if shift == 0 else pltpu.roll(x, shift, axis)


def inverse(x):
    guess = pl.reciprocal(x, approx=True)
    return guess * (2.0 - x * guess)


def lanes_of(shape):
    return lax.broadcasted_iota(jnp.int32, shape, len(shape) - 1)


def rows_of(shape):
    return lax.broadcasted_iota(jnp.int32, shape, len(shape) - 2)


def exchange_kernel(
    species, velocity, heat, vert, side, own, cells, own_v, out_v, load, send_v, recv_v, send_s, recv_s
):
    wn = lax.axis_index("wn")
    blk = lax.axis_index("blk")
    wn_count = lax.axis_size("wn")
    blk_count = lax.axis_size("blk")

    def exists(dw, db):
        checks = []
        if dw:
            checks.append(wn < wn_count - 1 if dw > 0 else wn > 0)
        if db:
            checks.append(blk < blk_count - 1 if db > 0 else blk > 0)
        return checks[0] if len(checks) == 1 else jnp.logical_and(*checks)

    def device(dw, db):
        return {"wn": wn + dw, "blk": blk + db}

    barrier = pltpu.get_barrier_semaphore()
    for dw, db in VERTICAL + SIDEWAYS:

        @pl.when(exists(dw, db))
        def _(dw=dw, db=db):
            pl.semaphore_signal(
                barrier, inc=1, device_id=device(dw, db), device_id_type=pl.DeviceIdType.MESH
            )

    loads = [
        pltpu.make_async_copy(species, cells.at[0:NS], load.at[0]),
        pltpu.make_async_copy(velocity, cells.at[NS:NS + 2], load.at[1]),
        pltpu.make_async_copy(heat, cells.at[NV - 1], load.at[2]),
    ]
    for copy in loads:
        copy.start()
    for copy in loads:
        copy.wait()

    def tile(v, g):
        return cells[v, pl.ds(8 * g, 8)]

    slot = lanes_of((8, 128)) // 8
    for t in range(EDGE_TILES):
        packed = jnp.zeros((8, 128), jnp.float32)
        for v in range(4 * t, min(4 * t + 4, NV)):
            for g in range(4):
                at = 4 * (v % 4) + g
                packed = jnp.where(slot == at, roll(tile(v, g), 8 * at + 3, 1), packed)
        own_v[t] = packed
        out_v[0, NV + t] = packed
        out_v[1, NV + t] = packed
    for v in range(NV):
        out_v[0, v] = tile(v, 3)
        out_v[1, v] = tile(v, 0)

    along_wn = 1 + (wn > 0).astype(jnp.int32) + (wn < wn_count - 1).astype(jnp.int32)
    along_blk = 1 + (blk > 0).astype(jnp.int32) + (blk < blk_count - 1).astype(jnp.int32)
    pl.semaphore_wait(barrier, along_wn * along_blk - 1)

    copies = []
    for n, (dw, db) in enumerate(VERTICAL):
        copies.append((dw, db, pltpu.make_async_remote_copy(
            src_ref=out_v.at[n], dst_ref=vert.at[n], send_sem=send_v.at[n], recv_sem=recv_v.at[n],
            device_id=device(dw, db), device_id_type=pl.DeviceIdType.MESH)))
    for n, (dw, db) in enumerate(SIDEWAYS):
        copies.append((dw, db, pltpu.make_async_remote_copy(
            src_ref=own_v, dst_ref=side.at[n], send_sem=send_s.at[n], recv_sem=recv_s.at[n],
            device_id=device(dw, db), device_id_type=pl.DeviceIdType.MESH)))
    for dw, db, copy in copies:
        pl.when(exists(dw, db))(copy.start)
    keep = pltpu.make_async_copy(own_v, own, load.at[3])
    keep.start()
    for dw, db, copy in copies:
        pl.when(exists(-dw, -db))(copy.wait_recv)
    for dw, db, copy in copies:
        pl.when(exists(dw, db))(copy.wait_send)
    keep.wait()


def sections_kernel(
    shear, thermal, species, velocity, heat, vert, side, own, final, residual, now, first, kept,
    edges, load
):
    moves = (
        (vert.at[0, NV:], edges.at[7]),
        (vert.at[1, NV:], edges.at[8]),
        (side, edges.at[0:6]),
        (own, edges.at[6]),
        (vert.at[0, 0:NV], now.at[:, 8:16]),
        (vert.at[1, 0:NV], now.at[:, 48:56]),
        (species, now.at[0:NS, 16:48]),
        (velocity, now.at[NS:NS + 2, 16:48]),
        (heat, now.at[NV - 1, 16:48]),
    )
    copies = [pltpu.make_async_copy(a, b, load.at[n]) for n, (a, b) in enumerate(moves)]
    for copy in copies:
        copy.start()
    wn = lax.axis_index("wn")
    blk = lax.axis_index("blk")
    at_bottom = wn == 0
    at_top = wn == lax.axis_size("wn") - 1
    at_wake = blk == 0
    at_nose = blk == lax.axis_size("blk") - 1
    lane = lanes_of((8, 128))
    sub = rows_of((8, 128))
    c = lane % 8
    is_left = lane < 64
    group = (lane % 64) // 8
    for copy in copies:
        copy.wait()

    for t in range(EDGE_TILES):
        from_left, from_right = c < 3, c >= 3
        mid, low, high = edges[6, t], edges[7, t], edges[8, t]
        left_mid = jnp.where(from_left, edges[0, t], mid)
        left_low = jnp.where(from_left, edges[2, t], low)
        left_high = jnp.where(from_left, edges[4, t], high)
        right_mid = jnp.where(from_right, edges[1, t], mid)
        right_low = jnp.where(from_right, edges[3, t], low)
        right_high = jnp.where(from_right, edges[5, t], high)
        for v in range(4 * t, min(4 * t + 4, NV)):
            base = 32 * (v % 4)
            left = roll(left_mid, 8 - base, 1)
            left = jnp.where(group == 0, roll(left_low, -24 - base, 1), left)
            left = jnp.where(group == 5, roll(left_high, 40 - base, 1), left)
            right = roll(right_mid, 72 - base, 1)
            right = jnp.where(group == 0, roll(right_low, 40 - base, 1), right)
            right = jnp.where(group == 5, roll(right_high, 104 - base, 1), right)
            now[v, 0:8] = jnp.where(is_left, left, right)
    first[...] = now[...]

    patch_bottom_6 = (sub == 6) & (group == 0)
    patch_bottom_7 = (sub == 7) & (group == 0)
    patch_top = (sub < 2) & (group == 5)
    patch_wake = is_left & (c == 2)
    patch_nose = (~is_left) & (c == 3)
    even = sub % 2 == 0

    def ghosts():
        @pl.when(at_bottom)
        def _():
            for v in range(NV):
                now[v, 14:15] = now[v, 19:20]
                now[v, 15:16] = now[v, 18:19]
                patch = now[v, 0:8]
                inner = roll(patch, -8, 1)
                patch = jnp.where(patch_bottom_6, roll(inner, 3, 0), patch)
                now[v, 0:8] = jnp.where(patch_bottom_7, roll(inner, 5, 0), patch)

        @pl.when(at_top)
        def _():
            for v in range(NV):
                now[v, 48:50] = now[v, 46:48]
                patch = now[v, 0:8]
                now[v, 0:8] = jnp.where(patch_top, roll(roll(patch, 8, 1), 2, 0), patch)

        @pl.when(at_wake)
        def _():
            for v in range(NV):
                patch = now[v, 0:8]
                now[v, 0:8] = jnp.where(patch_wake, roll(patch, -1, 1), patch)

        @pl.when(at_nose)
        def _():
            for v in range(NV):
                patch = now[v, 0:8]
                inner = roll(patch, 1, 1)
                inner = jnp.where(even, roll(inner, -1, 0), roll(inner, 1, 0))
                now[v, 0:8] = jnp.where(patch_nose, inner, patch)

    def patch_up(x):
        y = roll(x, -2, 0)
        return jnp.where(sub < 6, y, roll(y, -8, 1))

    def patch_down(x):
        y = roll(x, 2, 0)
        return jnp.where(sub >= 2, y, roll(y, 8, 1))

    def section(number, old_share, new_share):
        ghosts()
        if number == 0:
            cells = [now[r, 0:56] for r in range(NV)]
        else:
            cells = [
                jnp.concatenate(
                    [now[r, 0:8], now[r, 16:48], jnp.where(sub >= 4, now[r, 8:16], now[r, 48:56])],
                    axis=0,
                )
                for r in range(NV)
            ]
        visc = cond = None
        for s in range(NS):
            den_visc = shear[s, 0] * cells[0]
            den_cond = thermal[s, 0] * cells[0]
            for r in range(1, NS):
                den_visc = den_visc + shear[s, r] * cells[r]
                den_cond = den_cond + thermal[s, r] * cells[r]
            visc_s = (float(MASSES[s]) * cells[s]) * inverse(den_visc)
            cond_s = cells[s] * inverse(den_cond)
            visc = visc_s if s == 0 else visc + visc_s
            cond = cond_s if s == 0 else cond + cond_s
        temperature = cells[NV - 1]
        visc = jnp.exp(0.7 * jnp.log(temperature)) * visc
        cond = jnp.sqrt(temperature) * cond
        for n, k in enumerate((visc, cond)):
            if number == 0:
                kept[n, 0:56] = k
            else:
                kept[n, 0:8] = k[0:8]
                kept[n, 16:48] = k[8:40]
                kept[n, 8:16] = k[40:48]
                kept[n, 48:56] = k[40:48]
        for n in range(2):
            main, patch = kept[n, 8:56], kept[n, 0:8]
            kept[2 + n, 8:56] = 0.5 * (main + kept[n, 10:58])
            kept[2 + n, 0:8] = 0.5 * (patch + patch_up(patch))
            kept[4 + n, 8:56] = 0.5 * (main + roll(main, -1, 1))
            kept[4 + n, 0:8] = 0.5 * (patch + roll(patch, -1, 1))
        low, count = (8, 48) if number < 2 else (16, 32)
        here, after, ahead = pl.ds(low, count), pl.ds(low + 2, count), pl.ds(low - 2, count)
        last_lane = lanes_of((count, 128)) == 127
        zero_lane = lanes_of((count, 128)) == 0
        for v in range(NV):
            n = 0 if NS <= v < NS + 2 else 1
            main, patch = now[v, here], now[v, 0:8]
            across_patch = kept[4 + n, 0:8] * (roll(patch, -1, 1) - patch)
            seam = jnp.where(c == 1, roll(across_patch, 63, 1), across_patch)
            groups = range(low // 8 - 1, (low + count) // 8 - 1)
            closing = jnp.concatenate([roll(seam, -8 * g - 2, 1) for g in groups], axis=0)
            across = kept[4 + n, here] * (roll(main, -1, 1) - main)
            before = jnp.where(zero_lane, closing, roll(across, 1, 1))
            across = jnp.where(last_lane, closing, across)
            change = (across - before) + (
                kept[2 + n, here] * (now[v, after] - main)
                + kept[2 + n, ahead] * (now[v, ahead] - main)
            )
            if number < 2:
                down_patch = kept[2 + n, 0:8] * (patch_up(patch) - patch)
                change_patch = (across_patch - roll(across_patch, 1, 1)) + (
                    down_patch - patch_down(down_patch)
                )
                new_main = main + STEP * change
                new_patch = patch + STEP * change_patch
                if old_share:
                    new_main = old_share * first[v, here] + new_share * new_main
                    new_patch = old_share * first[v, 0:8] + new_share * new_patch
                now[v, here] = new_main
                now[v, 0:8] = new_patch
            else:
                residual[v] = change
                final[v] = old_share * first[v, here] + new_share * (main + STEP * change)

    section(0, 0.0, 1.0)
    section(1, 0.75, 0.25)
    section(2, 1.0 / 3.0, 2.0 / 3.0)


def local(species, velocity, heat, shear, thermal):
    layers = species.shape[1]
    columns = species.shape[3]
    assert (layers, columns) == (16, 128)
    rows = 2 * layers
    species = species.reshape(NS, rows, columns)
    velocity = velocity.reshape(2, rows, columns)
    heat = heat.reshape(rows, columns)
    f32 = jnp.float32
    vmem = pl.BlockSpec(memory_space=pltpu.VMEM)
    smem = pl.BlockSpec(memory_space=pltpu.SMEM)
    anywhere = pl.BlockSpec(memory_space=pl.ANY)
    tiles = NV + EDGE_TILES
    vert, side, own = pl.pallas_call(
        exchange_kernel,
        out_shape=(
            jax.ShapeDtypeStruct((2, tiles, 8, columns), f32),
            jax.ShapeDtypeStruct((6, EDGE_TILES, 8, columns), f32),
            jax.ShapeDtypeStruct((EDGE_TILES, 8, columns), f32),
        ),
        in_specs=[pl.BlockSpec(memory_space=pltpu.HBM)] * 3,
        out_specs=(anywhere,) * 3,
        scratch_shapes=[
            pltpu.VMEM((NV, rows, columns), f32),
            pltpu.VMEM((EDGE_TILES, 8, columns), f32),
            pltpu.VMEM((2, tiles, 8, columns), f32),
            pltpu.SemaphoreType.DMA((4,)),
            pltpu.SemaphoreType.DMA((2,)),
            pltpu.SemaphoreType.DMA((2,)),
            pltpu.SemaphoreType.DMA((6,)),
            pltpu.SemaphoreType.DMA((6,)),
        ],
        compiler_params=pltpu.CompilerParams(
            collective_id=0, has_side_effects=True, vmem_limit_bytes=8 * 2**20
        ),
        name="exchange",
    )(species, velocity, heat)
    shape = jax.ShapeDtypeStruct((NV, rows, columns), f32)
    final, residual = pl.pallas_call(
        sections_kernel,
        out_shape=(shape, shape),
        in_specs=[smem] * 2 + [anywhere] * 6,
        out_specs=(vmem,) * 2,
        scratch_shapes=[
            pltpu.VMEM((NV, rows + 32, columns), f32),
            pltpu.VMEM((NV, rows + 32, columns), f32),
            pltpu.VMEM((6, rows + 32, columns), f32),
            pltpu.VMEM((9, EDGE_TILES, 8, columns), f32),
            pltpu.SemaphoreType.DMA((9,)),
        ],
        compiler_params=pltpu.CompilerParams(vmem_limit_bytes=16 * 2**20),
        name="sections",
    )(shear, thermal, species, velocity, heat, vert, side, own)
    whole = (NV, layers, 2, columns)
    return final.reshape(whole), residual.reshape(whole)


def solution(mesh):
    return jax.shard_map(
        local,
        mesh=mesh,
        in_specs=(
            P(None, "wn", None, "blk"),
            P(None, "wn", None, "blk"),
            P("wn", None, "blk"),
            P(),
            P(),
        ),
        out_specs=(P(None, "wn", None, "blk"), P(None, "wn", None, "blk")),
        check_vma=False,
    )
```

```python
import jax
import jax.numpy as jnp
import numpy as np
from jax import lax
from jax.experimental import pallas as pl
from jax.experimental.pallas import tpu as pltpu
from jax.sharding import PartitionSpec as P

MASSES = np.array([28.0, 32.0, 30.0, 14.0, 16.0, 28.0, 32.0, 30.0, 14.0, 16.0, 0.00055]) / 28.0
NS = 11
NV = 14
STEP = 0.16
VERTICAL = ((1, 0), (-1, 0))
SIDEWAYS = ((0, 1), (0, -1), (1, 1), (1, -1), (-1, 1), (-1, -1))
EDGE_TILES = 4


def roll(x, shift, axis):
    size = x.shape[axis]
    shift = shift % size
    return x if shift == 0 else pltpu.roll(x, shift, axis)


def inverse(x):
    guess = pl.reciprocal(x, approx=True)
    return guess * (2.0 - x * guess)


def lanes_of(shape):
    return lax.broadcasted_iota(jnp.int32, shape, len(shape) - 1)


def rows_of(shape):
    return lax.broadcasted_iota(jnp.int32, shape, len(shape) - 2)


def exchange_kernel(
    species, velocity, heat, vert, side, own, cells, own_v, out_v, load, send_v, recv_v, send_s, recv_s
):
    wn = lax.axis_index("wn")
    blk = lax.axis_index("blk")
    wn_count = lax.axis_size("wn")
    blk_count = lax.axis_size("blk")

    def exists(dw, db):
        checks = []
        if dw:
            checks.append(wn < wn_count - 1 if dw > 0 else wn > 0)
        if db:
            checks.append(blk < blk_count - 1 if db > 0 else blk > 0)
        return checks[0] if len(checks) == 1 else jnp.logical_and(*checks)

    def device(dw, db):
        return {"wn": wn + dw, "blk": blk + db}

    barrier = pltpu.get_barrier_semaphore()
    for dw, db in VERTICAL + SIDEWAYS:

        @pl.when(exists(dw, db))
        def _(dw=dw, db=db):
            pl.semaphore_signal(
                barrier, inc=1, device_id=device(dw, db), device_id_type=pl.DeviceIdType.MESH
            )

    loads = [
        pltpu.make_async_copy(species, cells.at[0:NS], load.at[0]),
        pltpu.make_async_copy(velocity, cells.at[NS:NS + 2], load.at[1]),
        pltpu.make_async_copy(heat, cells.at[NV - 1], load.at[2]),
    ]
    for copy in loads:
        copy.start()
    for copy in loads:
        copy.wait()

    def tile(v, g):
        return cells[v, pl.ds(8 * g, 8)]

    slot = lanes_of((8, 128)) // 8
    for t in range(EDGE_TILES):
        packed = jnp.zeros((8, 128), jnp.float32)
        for v in range(4 * t, min(4 * t + 4, NV)):
            for g in range(4):
                at = 4 * (v % 4) + g
                packed = jnp.where(slot == at, roll(tile(v, g), 8 * at + 3, 1), packed)
        own_v[t] = packed
        out_v[0, NV + t] = packed
        out_v[1, NV + t] = packed
    for v in range(NV):
        out_v[0, v] = tile(v, 3)
        out_v[1, v] = tile(v, 0)

    along_wn = 1 + (wn > 0).astype(jnp.int32) + (wn < wn_count - 1).astype(jnp.int32)
    along_blk = 1 + (blk > 0).astype(jnp.int32) + (blk < blk_count - 1).astype(jnp.int32)
    pl.semaphore_wait(barrier, along_wn * along_blk - 1)

    copies = []
    for n, (dw, db) in enumerate(VERTICAL):
        copies.append((dw, db, pltpu.make_async_remote_copy(
            src_ref=out_v.at[n], dst_ref=vert.at[n], send_sem=send_v.at[n], recv_sem=recv_v.at[n],
            device_id=device(dw, db), device_id_type=pl.DeviceIdType.MESH)))
    for n, (dw, db) in enumerate(SIDEWAYS):
        copies.append((dw, db, pltpu.make_async_remote_copy(
            src_ref=own_v, dst_ref=side.at[n], send_sem=send_s.at[n], recv_sem=recv_s.at[n],
            device_id=device(dw, db), device_id_type=pl.DeviceIdType.MESH)))
    for dw, db, copy in copies:
        pl.when(exists(dw, db))(copy.start)
    keep = pltpu.make_async_copy(own_v, own, load.at[3])
    keep.start()
    for dw, db, copy in copies:
        pl.when(exists(-dw, -db))(copy.wait_recv)
    for dw, db, copy in copies:
        pl.when(exists(dw, db))(copy.wait_send)
    keep.wait()


def sections_kernel(
    shear, thermal, species, velocity, heat, vert, side, own, final, residual, now, first, kept
):
    wn = lax.axis_index("wn")
    blk = lax.axis_index("blk")
    at_bottom = wn == 0
    at_top = wn == lax.axis_size("wn") - 1
    at_wake = blk == 0
    at_nose = blk == lax.axis_size("blk") - 1
    lane = lanes_of((8, 128))
    sub = rows_of((8, 128))
    c = lane % 8
    is_left = lane < 64
    group = (lane % 64) // 8

    for v in range(NV):
        now[v, 0:8] = vert[0, v]
        now[v, 40:48] = vert[1, v]
    now[0:NS, 8:40] = species[...]
    now[NS:NS + 2, 8:40] = velocity[...]
    now[NV - 1, 8:40] = heat[...]
    for t in range(EDGE_TILES):
        from_left, from_right = c < 3, c >= 3
        mid, low, high = own[t], vert[0, NV + t], vert[1, NV + t]
        left_mid = jnp.where(from_left, side[0, t], mid)
        left_low = jnp.where(from_left, side[2, t], low)
        left_high = jnp.where(from_left, side[4, t], high)
        right_mid = jnp.where(from_right, side[1, t], mid)
        right_low = jnp.where(from_right, side[3, t], low)
        right_high = jnp.where(from_right, side[5, t], high)
        for v in range(4 * t, min(4 * t + 4, NV)):
            base = 32 * (v % 4)
            left = roll(left_mid, 8 - base, 1)
            left = jnp.where(group == 0, roll(left_low, -24 - base, 1), left)
            left = jnp.where(group == 5, roll(left_high, 40 - base, 1), left)
            right = roll(right_mid, 72 - base, 1)
            right = jnp.where(group == 0, roll(right_low, 40 - base, 1), right)
            right = jnp.where(group == 5, roll(right_high, 104 - base, 1), right)
            now[v, 48:56] = jnp.where(is_left, left, right)
    first[...] = now[...]

    bottom_6 = (sub == 6) & at_bottom
    bottom_7 = (sub == 7) & at_bottom
    top_01 = (sub < 2) & at_top
    patch_bottom_6 = bottom_6 & (group == 0)
    patch_bottom_7 = bottom_7 & (group == 0)
    patch_top = top_01 & (group == 5)
    patch_wake = is_left & (c == 2) & at_wake
    patch_nose = (~is_left) & (c == 3) & at_nose
    even = sub % 2 == 0

    def ghost(v):
        inner = now[v, 8:16]
        below = now[v, 0:8]
        below = jnp.where(bottom_6, roll(inner, 3, 0), below)
        now[v, 0:8] = jnp.where(bottom_7, roll(inner, 5, 0), below)
        now[v, 40:48] = jnp.where(top_01, roll(now[v, 32:40], 2, 0), now[v, 40:48])
        patch = now[v, 48:56]
        inner = roll(patch, -8, 1)
        patch = jnp.where(patch_bottom_6, roll(inner, 3, 0), patch)
        patch = jnp.where(patch_bottom_7, roll(inner, 5, 0), patch)
        patch = jnp.where(patch_top, roll(roll(patch, 8, 1), 2, 0), patch)
        patch = jnp.where(patch_wake, roll(patch, -1, 1), patch)
        inner = roll(patch, 1, 1)
        patch = jnp.where(
            patch_nose, jnp.where(even, roll(inner, -1, 0), roll(inner, 1, 0)), patch
        )
        now[v, 48:56] = patch

    def patch_up(x):
        y = roll(x, -2, 0)
        return jnp.where(sub < 6, y, roll(y, -8, 1))

    def patch_down(x):
        y = roll(x, 2, 0)
        return jnp.where(sub >= 2, y, roll(y, 8, 1))

    main_lane = lanes_of((48, 128))
    last_lane = main_lane == 127
    zero_lane = main_lane == 0

    def section(number, carry):
        old_share = jnp.where(number == 0, 0.0, jnp.where(number == 1, 0.75, 1.0 / 3.0))
        new_share = jnp.where(number == 0, 1.0, jnp.where(number == 1, 0.25, 2.0 / 3.0))
        for v in range(NV):
            ghost(v)
        cells = [now[r] for r in range(NV)]
        visc = cond = None
        for s in range(NS):
            den_visc = shear[s, 0] * cells[0]
            den_cond = thermal[s, 0] * cells[0]
            for r in range(1, NS):
                den_visc = den_visc + shear[s, r] * cells[r]
                den_cond = den_cond + thermal[s, r] * cells[r]
            visc_s = (float(MASSES[s]) * cells[s]) * inverse(den_visc)
            cond_s = cells[s] * inverse(den_cond)
            visc = visc_s if s == 0 else visc + visc_s
            cond = cond_s if s == 0 else cond + cond_s
        temperature = cells[NV - 1]
        visc = jnp.exp(0.7 * jnp.log(temperature)) * visc
        cond = jnp.sqrt(temperature) * cond
        for n, k in enumerate((visc, cond)):
            kept[n] = k
        for n in range(2):
            main, patch = kept[n, 0:48], kept[n, 48:56]
            kept[2 + n, 0:48] = 0.5 * (main + roll(main, -2, 0))
            kept[2 + n, 48:56] = 0.5 * (patch + patch_up(patch))
            kept[4 + n, 0:48] = 0.5 * (main + roll(main, -1, 1))
            kept[4 + n, 48:56] = 0.5 * (patch + roll(patch, -1, 1))
        for v in range(NV):
            n = 0 if NS <= v < NS + 2 else 1
            main, patch = now[v, 0:48], now[v, 48:56]
            across_patch = kept[4 + n, 48:56] * (roll(patch, -1, 1) - patch)
            seam = jnp.where(c == 1, roll(across_patch, 63, 1), across_patch)
            closing = jnp.concatenate([roll(seam, -8 * g - 2, 1) for g in range(6)], axis=0)
            across = kept[4 + n, 0:48] * (roll(main, -1, 1) - main)
            before = jnp.where(zero_lane, closing, roll(across, 1, 1))
            across = jnp.where(last_lane, closing, across)
            down = kept[2 + n, 0:48] * (roll(main, -2, 0) - main)
            change = (across - before) + (down - roll(down, 2, 0))
            down_patch = kept[2 + n, 48:56] * (patch_up(patch) - patch)
            change_patch = (across_patch - roll(across_patch, 1, 1)) + (
                down_patch - patch_down(down_patch)
            )
            new_main = old_share * first[v, 0:48] + new_share * (main + STEP * change)
            now[v, 0:48] = new_main
            now[v, 48:56] = old_share * first[v, 48:56] + new_share * (patch + STEP * change_patch)
            residual[v] = change[8:40]
            final[v] = new_main[8:40]
        return carry

    lax.fori_loop(0, 3, section, 0)


def local(species, velocity, heat, shear, thermal):
    layers = species.shape[1]
    columns = species.shape[3]
    assert (layers, columns) == (16, 128)
    rows = 2 * layers
    species = species.reshape(NS, rows, columns)
    velocity = velocity.reshape(2, rows, columns)
    heat = heat.reshape(rows, columns)
    f32 = jnp.float32
    vmem = pl.BlockSpec(memory_space=pltpu.VMEM)
    smem = pl.BlockSpec(memory_space=pltpu.SMEM)
    anywhere = pl.BlockSpec(memory_space=pl.ANY)
    tiles = NV + EDGE_TILES
    vert, side, own = pl.pallas_call(
        exchange_kernel,
        out_shape=(
            jax.ShapeDtypeStruct((2, tiles, 8, columns), f32),
            jax.ShapeDtypeStruct((6, EDGE_TILES, 8, columns), f32),
            jax.ShapeDtypeStruct((EDGE_TILES, 8, columns), f32),
        ),
        in_specs=[anywhere] * 3,
        out_specs=(anywhere,) * 3,
        scratch_shapes=[
            pltpu.VMEM((NV, rows, columns), f32),
            pltpu.VMEM((EDGE_TILES, 8, columns), f32),
            pltpu.VMEM((2, tiles, 8, columns), f32),
            pltpu.SemaphoreType.DMA((4,)),
            pltpu.SemaphoreType.DMA((2,)),
            pltpu.SemaphoreType.DMA((2,)),
            pltpu.SemaphoreType.DMA((6,)),
            pltpu.SemaphoreType.DMA((6,)),
        ],
        compiler_params=pltpu.CompilerParams(collective_id=0, has_side_effects=True),
        name="exchange",
    )(species, velocity, heat)
    shape = jax.ShapeDtypeStruct((NV, rows, columns), f32)
    final, residual = pl.pallas_call(
        sections_kernel,
        out_shape=(shape, shape),
        in_specs=[smem] * 2 + [vmem] * 6,
        out_specs=(vmem,) * 2,
        scratch_shapes=[
            pltpu.VMEM((NV, rows + 24, columns), f32),
            pltpu.VMEM((NV, rows + 24, columns), f32),
            pltpu.VMEM((6, rows + 24, columns), f32),
        ],
        name="sections",
    )(shear, thermal, species, velocity, heat, vert, side, own)
    whole = (NV, layers, 2, columns)
    return final.reshape(whole), residual.reshape(whole)


def solution(mesh):
    return jax.shard_map(
        local,
        mesh=mesh,
        in_specs=(
            P(None, "wn", None, "blk"),
            P(None, "wn", None, "blk"),
            P("wn", None, "blk"),
            P(),
            P(),
        ),
        out_specs=(P(None, "wn", None, "blk"), P(None, "wn", None, "blk")),
        check_vma=False,
    )
```

```python
import jax
import jax.numpy as jnp
import numpy as np
from jax import lax
from jax.experimental import pallas as pl
from jax.experimental.pallas import tpu as pltpu
from jax.sharding import PartitionSpec as P

MASSES = np.array([28.0, 32.0, 30.0, 14.0, 16.0, 28.0, 32.0, 30.0, 14.0, 16.0, 0.00055]) / 28.0
NS = 11
NV = 14
STEP = 0.16
VERTICAL = ((1, 0), (-1, 0))
SIDEWAYS = ((0, 1), (0, -1), (1, 1), (1, -1), (-1, 1), (-1, -1))
EDGE_TILES = 4


def roll(x, shift, axis):
    size = x.shape[axis]
    shift = shift % size
    return x if shift == 0 else pltpu.roll(x, shift, axis)


def inverse(x):
    guess = pl.reciprocal(x, approx=True)
    return guess * (2.0 - x * guess)


def lanes_of(shape):
    return lax.broadcasted_iota(jnp.int32, shape, len(shape) - 1)


def rows_of(shape):
    return lax.broadcasted_iota(jnp.int32, shape, len(shape) - 2)


def exchange_kernel(
    species, velocity, heat, vert, side, own, cells, own_v, out_v, load, send_v, recv_v, send_s, recv_s
):
    wn = lax.axis_index("wn")
    blk = lax.axis_index("blk")
    wn_count = lax.axis_size("wn")
    blk_count = lax.axis_size("blk")

    def exists(dw, db):
        checks = []
        if dw:
            checks.append(wn < wn_count - 1 if dw > 0 else wn > 0)
        if db:
            checks.append(blk < blk_count - 1 if db > 0 else blk > 0)
        return checks[0] if len(checks) == 1 else jnp.logical_and(*checks)

    def device(dw, db):
        return {"wn": wn + dw, "blk": blk + db}

    barrier = pltpu.get_barrier_semaphore()
    for dw, db in VERTICAL + SIDEWAYS:

        @pl.when(exists(dw, db))
        def _(dw=dw, db=db):
            pl.semaphore_signal(
                barrier, inc=1, device_id=device(dw, db), device_id_type=pl.DeviceIdType.MESH
            )

    loads = [
        pltpu.make_async_copy(species, cells.at[0:NS], load.at[0]),
        pltpu.make_async_copy(velocity, cells.at[NS:NS + 2], load.at[1]),
        pltpu.make_async_copy(heat, cells.at[NV - 1], load.at[2]),
    ]
    for copy in loads:
        copy.start()
    for copy in loads:
        copy.wait()

    def tile(v, g):
        return cells[v, pl.ds(8 * g, 8)]

    slot = lanes_of((8, 128)) // 8
    for t in range(EDGE_TILES):
        packed = jnp.zeros((8, 128), jnp.float32)
        for v in range(4 * t, min(4 * t + 4, NV)):
            for g in range(4):
                at = 4 * (v % 4) + g
                packed = jnp.where(slot == at, roll(tile(v, g), 8 * at + 3, 1), packed)
        own_v[t] = packed
        out_v[0, NV + t] = packed
        out_v[1, NV + t] = packed
    for v in range(NV):
        out_v[0, v] = tile(v, 3)
        out_v[1, v] = tile(v, 0)

    along_wn = 1 + (wn > 0).astype(jnp.int32) + (wn < wn_count - 1).astype(jnp.int32)
    along_blk = 1 + (blk > 0).astype(jnp.int32) + (blk < blk_count - 1).astype(jnp.int32)
    pl.semaphore_wait(barrier, along_wn * along_blk - 1)

    copies = []
    for n, (dw, db) in enumerate(VERTICAL):
        copies.append((dw, db, pltpu.make_async_remote_copy(
            src_ref=out_v.at[n], dst_ref=vert.at[n], send_sem=send_v.at[n], recv_sem=recv_v.at[n],
            device_id=device(dw, db), device_id_type=pl.DeviceIdType.MESH)))
    for n, (dw, db) in enumerate(SIDEWAYS):
        copies.append((dw, db, pltpu.make_async_remote_copy(
            src_ref=own_v, dst_ref=side.at[n], send_sem=send_s.at[n], recv_sem=recv_s.at[n],
            device_id=device(dw, db), device_id_type=pl.DeviceIdType.MESH)))
    for dw, db, copy in copies:
        pl.when(exists(dw, db))(copy.start)
    keep = pltpu.make_async_copy(own_v, own, load.at[3])
    keep.start()
    for dw, db, copy in copies:
        pl.when(exists(-dw, -db))(copy.wait_recv)
    for dw, db, copy in copies:
        pl.when(exists(dw, db))(copy.wait_send)
    keep.wait()


def sections_kernel(
    shear, thermal, species, velocity, heat, vert, side, own, final, residual, now, first, kept
):
    wn = lax.axis_index("wn")
    blk = lax.axis_index("blk")
    at_bottom = wn == 0
    at_top = wn == lax.axis_size("wn") - 1
    at_wake = blk == 0
    at_nose = blk == lax.axis_size("blk") - 1
    lane = lanes_of((8, 128))
    sub = rows_of((8, 128))
    c = lane % 8
    is_left = lane < 64
    group = (lane % 64) // 8

    for v in range(NV):
        now[v, 0:8] = vert[0, v]
        now[v, 40:48] = vert[1, v]
    now[0:NS, 8:40] = species[...]
    now[NS:NS + 2, 8:40] = velocity[...]
    now[NV - 1, 8:40] = heat[...]
    for t in range(EDGE_TILES):
        from_left, from_right = c < 3, c >= 3
        mid, low, high = own[t], vert[0, NV + t], vert[1, NV + t]
        left_mid = jnp.where(from_left, side[0, t], mid)
        left_low = jnp.where(from_left, side[2, t], low)
        left_high = jnp.where(from_left, side[4, t], high)
        right_mid = jnp.where(from_right, side[1, t], mid)
        right_low = jnp.where(from_right, side[3, t], low)
        right_high = jnp.where(from_right, side[5, t], high)
        for v in range(4 * t, min(4 * t + 4, NV)):
            base = 32 * (v % 4)
            left = roll(left_mid, 8 - base, 1)
            left = jnp.where(group == 0, roll(left_low, -24 - base, 1), left)
            left = jnp.where(group == 5, roll(left_high, 40 - base, 1), left)
            right = roll(right_mid, 72 - base, 1)
            right = jnp.where(group == 0, roll(right_low, 40 - base, 1), right)
            right = jnp.where(group == 5, roll(right_high, 104 - base, 1), right)
            now[v, 48:56] = jnp.where(is_left, left, right)
    first[...] = now[...]

    bottom_6 = (sub == 6) & at_bottom
    bottom_7 = (sub == 7) & at_bottom
    top_01 = (sub < 2) & at_top
    patch_bottom_6 = bottom_6 & (group == 0)
    patch_bottom_7 = bottom_7 & (group == 0)
    patch_top = top_01 & (group == 5)
    patch_wake = is_left & (c == 2) & at_wake
    patch_nose = (~is_left) & (c == 3) & at_nose
    even = sub % 2 == 0

    def ghost(v):
        inner = now[v, 8:16]
        below = now[v, 0:8]
        below = jnp.where(bottom_6, roll(inner, 3, 0), below)
        now[v, 0:8] = jnp.where(bottom_7, roll(inner, 5, 0), below)
        now[v, 40:48] = jnp.where(top_01, roll(now[v, 32:40], 2, 0), now[v, 40:48])
        patch = now[v, 48:56]
        inner = roll(patch, -8, 1)
        patch = jnp.where(patch_bottom_6, roll(inner, 3, 0), patch)
        patch = jnp.where(patch_bottom_7, roll(inner, 5, 0), patch)
        patch = jnp.where(patch_top, roll(roll(patch, 8, 1), 2, 0), patch)
        patch = jnp.where(patch_wake, roll(patch, -1, 1), patch)
        inner = roll(patch, 1, 1)
        patch = jnp.where(
            patch_nose, jnp.where(even, roll(inner, -1, 0), roll(inner, 1, 0)), patch
        )
        now[v, 48:56] = patch

    def patch_up(x):
        y = roll(x, -2, 0)
        return jnp.where(sub < 6, y, roll(y, -8, 1))

    def patch_down(x):
        y = roll(x, 2, 0)
        return jnp.where(sub >= 2, y, roll(y, 8, 1))

    main_lane = lanes_of((48, 128))
    last_lane = main_lane == 127
    zero_lane = main_lane == 0

    def section(number, old_share, new_share):
        for v in range(NV):
            ghost(v)
        if number == 0:
            cells = [now[r] for r in range(NV)]
        else:
            cells = [
                jnp.concatenate(
                    [now[r, 8:40], now[r, 48:56], jnp.where(sub >= 4, now[r, 0:8], now[r, 40:48])],
                    axis=0,
                )
                for r in range(NV)
            ]
        visc = cond = None
        for s in range(NS):
            den_visc = shear[s, 0] * cells[0]
            den_cond = thermal[s, 0] * cells[0]
            for r in range(1, NS):
                den_visc = den_visc + shear[s, r] * cells[r]
                den_cond = den_cond + thermal[s, r] * cells[r]
            visc_s = (float(MASSES[s]) * cells[s]) * inverse(den_visc)
            cond_s = cells[s] * inverse(den_cond)
            visc = visc_s if s == 0 else visc + visc_s
            cond = cond_s if s == 0 else cond + cond_s
        temperature = cells[NV - 1]
        visc = jnp.exp(0.7 * jnp.log(temperature)) * visc
        cond = jnp.sqrt(temperature) * cond
        for n, k in enumerate((visc, cond)):
            if number == 0:
                kept[n] = k
            else:
                kept[n, 8:40] = k[0:32]
                kept[n, 48:56] = k[32:40]
                kept[n, 0:8] = k[40:48]
                kept[n, 40:48] = k[40:48]
        for n in range(2):
            main, patch = kept[n, 0:48], kept[n, 48:56]
            kept[2 + n, 0:48] = 0.5 * (main + roll(main, -2, 0))
            kept[2 + n, 48:56] = 0.5 * (patch + patch_up(patch))
            kept[4 + n, 0:48] = 0.5 * (main + roll(main, -1, 1))
            kept[4 + n, 48:56] = 0.5 * (patch + roll(patch, -1, 1))
        for v in range(NV):
            n = 0 if NS <= v < NS + 2 else 1
            main, patch = now[v, 0:48], now[v, 48:56]
            across_patch = kept[4 + n, 48:56] * (roll(patch, -1, 1) - patch)
            seam = jnp.where(c == 1, roll(across_patch, 63, 1), across_patch)
            closing = jnp.concatenate([roll(seam, -8 * g - 2, 1) for g in range(6)], axis=0)
            across = kept[4 + n, 0:48] * (roll(main, -1, 1) - main)
            before = jnp.where(zero_lane, closing, roll(across, 1, 1))
            across = jnp.where(last_lane, closing, across)
            down = kept[2 + n, 0:48] * (roll(main, -2, 0) - main)
            change = (across - before) + (down - roll(down, 2, 0))
            if number < 2:
                down_patch = kept[2 + n, 48:56] * (patch_up(patch) - patch)
                change_patch = (across_patch - roll(across_patch, 1, 1)) + (
                    down_patch - patch_down(down_patch)
                )
                new_main = main + STEP * change
                new_patch = patch + STEP * change_patch
                if old_share:
                    new_main = old_share * first[v, 0:48] + new_share * new_main
                    new_patch = old_share * first[v, 48:56] + new_share * new_patch
                now[v, 0:48] = new_main
                now[v, 48:56] = new_patch
            else:
                inner = change[8:40]
                residual[v] = inner
                final[v] = old_share * first[v, 8:40] + new_share * (main[8:40] + STEP * inner)

    section(0, 0.0, 1.0)
    section(1, 0.75, 0.25)
    section(2, 1.0 / 3.0, 2.0 / 3.0)


def local(species, velocity, heat, shear, thermal):
    layers = species.shape[1]
    columns = species.shape[3]
    assert (layers, columns) == (16, 128)
    rows = 2 * layers
    species = species.reshape(NS, rows, columns)
    velocity = velocity.reshape(2, rows, columns)
    heat = heat.reshape(rows, columns)
    f32 = jnp.float32
    vmem = pl.BlockSpec(memory_space=pltpu.VMEM)
    smem = pl.BlockSpec(memory_space=pltpu.SMEM)
    anywhere = pl.BlockSpec(memory_space=pl.ANY)
    tiles = NV + EDGE_TILES
    vert, side, own = pl.pallas_call(
        exchange_kernel,
        out_shape=(
            jax.ShapeDtypeStruct((2, tiles, 8, columns), f32),
            jax.ShapeDtypeStruct((6, EDGE_TILES, 8, columns), f32),
            jax.ShapeDtypeStruct((EDGE_TILES, 8, columns), f32),
        ),
        in_specs=[anywhere] * 3,
        out_specs=(anywhere,) * 3,
        scratch_shapes=[
            pltpu.VMEM((NV, rows, columns), f32),
            pltpu.VMEM((EDGE_TILES, 8, columns), f32),
            pltpu.VMEM((2, tiles, 8, columns), f32),
            pltpu.SemaphoreType.DMA((4,)),
            pltpu.SemaphoreType.DMA((2,)),
            pltpu.SemaphoreType.DMA((2,)),
            pltpu.SemaphoreType.DMA((6,)),
            pltpu.SemaphoreType.DMA((6,)),
        ],
        compiler_params=pltpu.CompilerParams(collective_id=0, has_side_effects=True),
        name="exchange",
    )(species, velocity, heat)
    shape = jax.ShapeDtypeStruct((NV, rows, columns), f32)
    final, residual = pl.pallas_call(
        sections_kernel,
        out_shape=(shape, shape),
        in_specs=[smem] * 2 + [vmem] * 6,
        out_specs=(vmem,) * 2,
        scratch_shapes=[
            pltpu.VMEM((NV, rows + 24, columns), f32),
            pltpu.VMEM((NV, rows + 24, columns), f32),
            pltpu.VMEM((6, rows + 24, columns), f32),
        ],
        name="sections",
    )(shear, thermal, species, velocity, heat, vert, side, own)
    whole = (NV, layers, 2, columns)
    return final.reshape(whole), residual.reshape(whole)


def solution(mesh):
    return jax.shard_map(
        local,
        mesh=mesh,
        in_specs=(
            P(None, "wn", None, "blk"),
            P(None, "wn", None, "blk"),
            P("wn", None, "blk"),
            P(),
            P(),
        ),
        out_specs=(P(None, "wn", None, "blk"), P(None, "wn", None, "blk")),
        check_vma=False,
    )
```

```python
import jax
import jax.numpy as jnp
import numpy as np
from jax import lax
from jax.experimental import pallas as pl
from jax.experimental.pallas import tpu as pltpu
from jax.sharding import PartitionSpec as P

MASSES = np.array([28.0, 32.0, 30.0, 14.0, 16.0, 28.0, 32.0, 30.0, 14.0, 16.0, 0.00055]) / 28.0
NS = 11
NV = 14
STEP = 0.16
VERTICAL = ((1, 0), (-1, 0))
SIDEWAYS = ((0, 1), (0, -1), (1, 1), (1, -1), (-1, 1), (-1, -1))
EDGE_TILES = 4


def roll(x, shift, axis):
    size = x.shape[axis]
    shift = shift % size
    return x if shift == 0 else pltpu.roll(x, shift, axis)


def inverse(x):
    guess = pl.reciprocal(x, approx=True)
    return guess * (2.0 - x * guess)


def lanes_of(shape):
    return lax.broadcasted_iota(jnp.int32, shape, len(shape) - 1)


def rows_of(shape):
    return lax.broadcasted_iota(jnp.int32, shape, len(shape) - 2)


def exchange_kernel(
    species, velocity, heat, vert, side, own, cells, own_v, out_v, load, send_v, recv_v, send_s, recv_s
):
    wn = lax.axis_index("wn")
    blk = lax.axis_index("blk")
    wn_count = lax.axis_size("wn")
    blk_count = lax.axis_size("blk")

    def exists(dw, db):
        checks = []
        if dw:
            checks.append(wn < wn_count - 1 if dw > 0 else wn > 0)
        if db:
            checks.append(blk < blk_count - 1 if db > 0 else blk > 0)
        return checks[0] if len(checks) == 1 else jnp.logical_and(*checks)

    def device(dw, db):
        return {"wn": wn + dw, "blk": blk + db}

    barrier = pltpu.get_barrier_semaphore()
    for dw, db in VERTICAL + SIDEWAYS:

        @pl.when(exists(dw, db))
        def _(dw=dw, db=db):
            pl.semaphore_signal(
                barrier, inc=1, device_id=device(dw, db), device_id_type=pl.DeviceIdType.MESH
            )

    loads = [
        pltpu.make_async_copy(species, cells.at[0:NS], load.at[0]),
        pltpu.make_async_copy(velocity, cells.at[NS:NS + 2], load.at[1]),
        pltpu.make_async_copy(heat, cells.at[NV - 1], load.at[2]),
    ]
    for copy in loads:
        copy.start()
    for copy in loads:
        copy.wait()

    def tile(v, g):
        return cells[v, pl.ds(8 * g, 8)]

    slot = lanes_of((8, 128)) // 8
    for t in range(EDGE_TILES):
        packed = jnp.zeros((8, 128), jnp.float32)
        for v in range(4 * t, min(4 * t + 4, NV)):
            for g in range(4):
                at = 4 * (v % 4) + g
                packed = jnp.where(slot == at, roll(tile(v, g), 8 * at + 3, 1), packed)
        own_v[t] = packed
        out_v[0, NV + t] = packed
        out_v[1, NV + t] = packed
    for v in range(NV):
        out_v[0, v] = tile(v, 3)
        out_v[1, v] = tile(v, 0)

    along_wn = 1 + (wn > 0).astype(jnp.int32) + (wn < wn_count - 1).astype(jnp.int32)
    along_blk = 1 + (blk > 0).astype(jnp.int32) + (blk < blk_count - 1).astype(jnp.int32)
    pl.semaphore_wait(barrier, along_wn * along_blk - 1)

    copies = []
    for n, (dw, db) in enumerate(VERTICAL):
        copies.append((dw, db, pltpu.make_async_remote_copy(
            src_ref=out_v.at[n], dst_ref=vert.at[n], send_sem=send_v.at[n], recv_sem=recv_v.at[n],
            device_id=device(dw, db), device_id_type=pl.DeviceIdType.MESH)))
    for n, (dw, db) in enumerate(SIDEWAYS):
        copies.append((dw, db, pltpu.make_async_remote_copy(
            src_ref=own_v, dst_ref=side.at[n], send_sem=send_s.at[n], recv_sem=recv_s.at[n],
            device_id=device(dw, db), device_id_type=pl.DeviceIdType.MESH)))
    for dw, db, copy in copies:
        pl.when(exists(dw, db))(copy.start)
    keep = pltpu.make_async_copy(own_v, own, load.at[3])
    keep.start()
    for dw, db, copy in copies:
        pl.when(exists(-dw, -db))(copy.wait_recv)
    for dw, db, copy in copies:
        pl.when(exists(dw, db))(copy.wait_send)
    keep.wait()


def sections_kernel(
    shear, thermal, species, velocity, heat, vert, side, own, final, residual, now, first, kept,
    final_v, residual_v, out
):
    wn = lax.axis_index("wn")
    blk = lax.axis_index("blk")
    at_bottom = wn == 0
    at_top = wn == lax.axis_size("wn") - 1
    at_wake = blk == 0
    at_nose = blk == lax.axis_size("blk") - 1
    lane = lanes_of((8, 128))
    sub = rows_of((8, 128))
    c = lane % 8
    is_left = lane < 64
    group = (lane % 64) // 8

    for v in range(NV):
        now[v, 0:8] = vert[0, v]
        now[v, 40:48] = vert[1, v]
    now[0:NS, 8:40] = species[...]
    now[NS:NS + 2, 8:40] = velocity[...]
    now[NV - 1, 8:40] = heat[...]
    for t in range(EDGE_TILES):
        from_left, from_right = c < 3, c >= 3
        mid, low, high = own[t], vert[0, NV + t], vert[1, NV + t]
        left_mid = jnp.where(from_left, side[0, t], mid)
        left_low = jnp.where(from_left, side[2, t], low)
        left_high = jnp.where(from_left, side[4, t], high)
        right_mid = jnp.where(from_right, side[1, t], mid)
        right_low = jnp.where(from_right, side[3, t], low)
        right_high = jnp.where(from_right, side[5, t], high)
        for v in range(4 * t, min(4 * t + 4, NV)):
            base = 32 * (v % 4)
            left = roll(left_mid, 8 - base, 1)
            left = jnp.where(group == 0, roll(left_low, -24 - base, 1), left)
            left = jnp.where(group == 5, roll(left_high, 40 - base, 1), left)
            right = roll(right_mid, 72 - base, 1)
            right = jnp.where(group == 0, roll(right_low, 40 - base, 1), right)
            right = jnp.where(group == 5, roll(right_high, 104 - base, 1), right)
            now[v, 48:56] = jnp.where(is_left, left, right)
    first[...] = now[...]

    bottom_6 = (sub == 6) & at_bottom
    bottom_7 = (sub == 7) & at_bottom
    top_01 = (sub < 2) & at_top
    patch_bottom_6 = bottom_6 & (group == 0)
    patch_bottom_7 = bottom_7 & (group == 0)
    patch_top = top_01 & (group == 5)
    patch_wake = is_left & (c == 2) & at_wake
    patch_nose = (~is_left) & (c == 3) & at_nose
    even = sub % 2 == 0

    def ghost(v):
        inner = now[v, 8:16]
        below = now[v, 0:8]
        below = jnp.where(bottom_6, roll(inner, 3, 0), below)
        now[v, 0:8] = jnp.where(bottom_7, roll(inner, 5, 0), below)
        now[v, 40:48] = jnp.where(top_01, roll(now[v, 32:40], 2, 0), now[v, 40:48])
        patch = now[v, 48:56]
        inner = roll(patch, -8, 1)
        patch = jnp.where(patch_bottom_6, roll(inner, 3, 0), patch)
        patch = jnp.where(patch_bottom_7, roll(inner, 5, 0), patch)
        patch = jnp.where(patch_top, roll(roll(patch, 8, 1), 2, 0), patch)
        patch = jnp.where(patch_wake, roll(patch, -1, 1), patch)
        inner = roll(patch, 1, 1)
        patch = jnp.where(
            patch_nose, jnp.where(even, roll(inner, -1, 0), roll(inner, 1, 0)), patch
        )
        now[v, 48:56] = patch

    def patch_up(x):
        y = roll(x, -2, 0)
        return jnp.where(sub < 6, y, roll(y, -8, 1))

    def patch_down(x):
        y = roll(x, 2, 0)
        return jnp.where(sub >= 2, y, roll(y, 8, 1))

    main_lane = lanes_of((48, 128))
    last_lane = main_lane == 127
    zero_lane = main_lane == 0

    def section(number, old_share, new_share):
        for v in range(NV):
            ghost(v)
        if number == 0:
            cells = [now[r] for r in range(NV)]
        else:
            cells = [
                jnp.concatenate(
                    [now[r, 8:40], now[r, 48:56], jnp.where(sub >= 4, now[r, 0:8], now[r, 40:48])],
                    axis=0,
                )
                for r in range(NV)
            ]
        visc = cond = None
        for s in range(NS):
            den_visc = shear[s, 0] * cells[0]
            den_cond = thermal[s, 0] * cells[0]
            for r in range(1, NS):
                den_visc = den_visc + shear[s, r] * cells[r]
                den_cond = den_cond + thermal[s, r] * cells[r]
            visc_s = (float(MASSES[s]) * cells[s]) * inverse(den_visc)
            cond_s = cells[s] * inverse(den_cond)
            visc = visc_s if s == 0 else visc + visc_s
            cond = cond_s if s == 0 else cond + cond_s
        temperature = cells[NV - 1]
        visc = jnp.exp(0.7 * jnp.log(temperature)) * visc
        cond = jnp.sqrt(temperature) * cond
        for n, k in enumerate((visc, cond)):
            if number == 0:
                kept[n] = k
            else:
                kept[n, 8:40] = k[0:32]
                kept[n, 48:56] = k[32:40]
                kept[n, 0:8] = k[40:48]
                kept[n, 40:48] = k[40:48]
        for n in range(2):
            main, patch = kept[n, 0:48], kept[n, 48:56]
            kept[2 + n, 0:48] = 0.5 * (main + roll(main, -2, 0))
            kept[2 + n, 48:56] = 0.5 * (patch + patch_up(patch))
            kept[4 + n, 0:48] = 0.5 * (main + roll(main, -1, 1))
            kept[4 + n, 48:56] = 0.5 * (patch + roll(patch, -1, 1))
        for v in range(NV):
            n = 0 if NS <= v < NS + 2 else 1
            main, patch = now[v, 0:48], now[v, 48:56]
            across_patch = kept[4 + n, 48:56] * (roll(patch, -1, 1) - patch)
            seam = jnp.where(c == 1, roll(across_patch, 63, 1), across_patch)
            closing = jnp.concatenate([roll(seam, -8 * g - 2, 1) for g in range(6)], axis=0)
            across = kept[4 + n, 0:48] * (roll(main, -1, 1) - main)
            before = jnp.where(zero_lane, closing, roll(across, 1, 1))
            across = jnp.where(last_lane, closing, across)
            down = kept[2 + n, 0:48] * (roll(main, -2, 0) - main)
            change = (across - before) + (down - roll(down, 2, 0))
            if number < 2:
                down_patch = kept[2 + n, 48:56] * (patch_up(patch) - patch)
                change_patch = (across_patch - roll(across_patch, 1, 1)) + (
                    down_patch - patch_down(down_patch)
                )
                new_main = main + STEP * change
                new_patch = patch + STEP * change_patch
                if old_share:
                    new_main = old_share * first[v, 0:48] + new_share * new_main
                    new_patch = old_share * first[v, 48:56] + new_share * new_patch
                now[v, 0:48] = new_main
                now[v, 48:56] = new_patch
            else:
                inner = change[8:40]
                residual_v[v] = inner
                final_v[v] = old_share * first[v, 8:40] + new_share * (main[8:40] + STEP * inner)
                if v in (3, 7, 10, 13):
                    n = len(leaving)
                    done = pl.ds((0, 4, 8, 11)[n // 2], (4, 4, 3, 3)[n // 2])
                    for here, there in ((final_v, final), (residual_v, residual)):
                        leaving.append(pltpu.make_async_copy(
                            here.at[done], there.at[done], out.at[len(leaving)]))
                        leaving[-1].start()

    leaving = []
    section(0, 0.0, 1.0)
    section(1, 0.75, 0.25)
    section(2, 1.0 / 3.0, 2.0 / 3.0)
    for copy in leaving:
        copy.wait()


def local(species, velocity, heat, shear, thermal):
    layers = species.shape[1]
    columns = species.shape[3]
    assert (layers, columns) == (16, 128)
    rows = 2 * layers
    species = species.reshape(NS, rows, columns)
    velocity = velocity.reshape(2, rows, columns)
    heat = heat.reshape(rows, columns)
    f32 = jnp.float32
    vmem = pl.BlockSpec(memory_space=pltpu.VMEM)
    smem = pl.BlockSpec(memory_space=pltpu.SMEM)
    anywhere = pl.BlockSpec(memory_space=pl.ANY)
    tiles = NV + EDGE_TILES
    vert, side, own = pl.pallas_call(
        exchange_kernel,
        out_shape=(
            jax.ShapeDtypeStruct((2, tiles, 8, columns), f32),
            jax.ShapeDtypeStruct((6, EDGE_TILES, 8, columns), f32),
            jax.ShapeDtypeStruct((EDGE_TILES, 8, columns), f32),
        ),
        in_specs=[anywhere] * 3,
        out_specs=(anywhere,) * 3,
        scratch_shapes=[
            pltpu.VMEM((NV, rows, columns), f32),
            pltpu.VMEM((EDGE_TILES, 8, columns), f32),
            pltpu.VMEM((2, tiles, 8, columns), f32),
            pltpu.SemaphoreType.DMA((4,)),
            pltpu.SemaphoreType.DMA((2,)),
            pltpu.SemaphoreType.DMA((2,)),
            pltpu.SemaphoreType.DMA((6,)),
            pltpu.SemaphoreType.DMA((6,)),
        ],
        compiler_params=pltpu.CompilerParams(collective_id=0, has_side_effects=True),
        name="exchange",
    )(species, velocity, heat)
    shape = jax.ShapeDtypeStruct((NV, rows, columns), f32)
    final, residual = pl.pallas_call(
        sections_kernel,
        out_shape=(shape, shape),
        in_specs=[smem] * 2 + [vmem] * 6,
        out_specs=(anywhere,) * 2,
        scratch_shapes=[
            pltpu.VMEM((NV, rows + 24, columns), f32),
            pltpu.VMEM((NV, rows + 24, columns), f32),
            pltpu.VMEM((6, rows + 24, columns), f32),
            pltpu.VMEM((NV, rows, columns), f32),
            pltpu.VMEM((NV, rows, columns), f32),
            pltpu.SemaphoreType.DMA((8,)),
        ],
        name="sections",
    )(shear, thermal, species, velocity, heat, vert, side, own)
    whole = (NV, layers, 2, columns)
    return final.reshape(whole), residual.reshape(whole)


def solution(mesh):
    return jax.shard_map(
        local,
        mesh=mesh,
        in_specs=(
            P(None, "wn", None, "blk"),
            P(None, "wn", None, "blk"),
            P("wn", None, "blk"),
            P(),
            P(),
        ),
        out_specs=(P(None, "wn", None, "blk"), P(None, "wn", None, "blk")),
        check_vma=False,
    )
```
